128 devices in a mesh: band: 8 (over y, core), order: 16 (over z, x).
Axes of the slice: x: 4, y: 4, z: 4, core: 2. Of those that a mesh axis runs over, the one named last changes fastest.
Arguments:
- thickness: float32 [2097152], P(('band', 'order')), may hold values from -24 to 24
- tile_weights: float32 [16384, 128, 128], P(('band', 'order')), may hold values from -0.5 to 0.5
- tile_dest: int32 [16384, 1], P(('band', 'order')), may hold values from 0 to 127; in each aligned block of 128 rows (0 to 127, 128 to 255, ...) at most 2 rows name the same one
- tile_row: int32 [16384], P(('band', 'order')), may hold values from 0 to 31
- tile_col: int32 [16384], P(('band', 'order')), may hold values from 0 to 63
- window: int32 [16], replicated, may hold values from 0 to 4095, as said below
- quad_weights: float32 [4096], P('band'), may hold values from 0.5 to 2
- legendre: float32 [16, 4096, 4096], P('order', 'band'), may hold values from -0.09375 to 0.09375
- love_code: int32 [4096], replicated, may hold values from 100 to 2000
Outputs:
- uplift: float32 [2097152], P(('band', 'order'))
- coefficients: float32 [16, 2, 4096], P('order')
The draws below stay inside these ranges and needn't reach their ends.
Inputs may be any that keep to these rules, and one draw needn't show every extreme that they name: `window`: the orders are distinct and below 4096; both 0 and 4095 are among them. `tile_dest`: among the tiles of one device, at most 2 have the same owner.
All inputs are finite; a program needn't handle non-finite values.
Results may differ from the reference program's by a relative error of at most 0.000098.
Values sent between devices are 32-bit elements; how exact they have to be, the bound alone decides.
A program may use at most 64 MiB of HBM per device.

```python
import math
import jax
import jax.numpy as jnp
import numpy as np
from jax import lax

NLAT = 4096
NLON = 8192
LDEG = 4096
TILES_DEV = 128
ORDERS = 16
TILES = 16384
ELEMS = 2097152
LAT_DEV = 32
CAP = 2
DEVICES = 128


def draw_window(key, part):
    half = NLON // 2
    inner = 1 + jax.random.permutation(jax.random.fold_in(key, 11), half - 2)[:ORDERS - 2]
    picked = jnp.concatenate([jnp.array([0, half - 1], jnp.int32), inner.astype(jnp.int32)])
    shuffle = jax.random.permutation(jax.random.fold_in(key, 12), ORDERS)
    return picked[shuffle]


def place_ends(entries, stream_key, smallest, top_value):
    longest = entries.shape.index(max(entries.shape))
    spots = []
    for shift in (0, 1):
        where = [jax.random.randint(jax.random.fold_in(stream_key, axis), (), 0, length) for axis, length in enumerate(entries.shape)]
        where[longest] = (where[longest] + shift) % entries.shape[longest]
        spots.append(tuple(where))
    return entries.at[spots[0]].set(smallest).at[spots[1]].set(top_value)


def block_levels(rng, extent, shards, smallest, largest):
    def one(position, shards_of):
        heights = jax.random.uniform(jax.random.fold_in(jax.random.fold_in(rng, 6), position), (shards_of,), jnp.float32, smallest / len(shards), largest / len(shards))
        return jnp.repeat(jnp.exp(heights), extent[position] // shards_of).reshape((-1,) + (1,) * (len(extent) - position - 1))

    level = one(*shards[0])
    for cut in shards[1:]:
        level = level * one(*cut)
    return level


def shared_out(stream_key, own, number, rows, number_of, top, limit, lean):
    order = jax.random.permutation(stream_key, number_of)
    crowded, common = shares(number_of, rows * top, limit, lean, True), shares(number_of, rows * top, limit, lean, False)
    places = jnp.arange(number_of)

    def named(sizes, rotation):
        used = int((sizes > 0).sum())
        fixed = max(1, used // 4)
        passed = fixed + (places - fixed + rotation * (used - fixed)) % max(1, number_of - fixed)
        return jnp.zeros((number_of,), jnp.int32).at[order[jnp.where(places < fixed, places, passed)]].set(jnp.asarray(sizes, jnp.int32))

    sizes = jnp.where(number % 4 == 0, named(crowded, number // 4), named(common, number - number // 4 - 1))
    mixed = jax.random.permutation(jax.random.fold_in(own, 3), number_of)
    source_of, taker = mixed[0:number_of // 2 * 2:2], mixed[1:number_of // 2 * 2:2]
    slack = jnp.minimum(sizes[source_of] - 1, limit - sizes[taker]) // 2
    slack = jnp.where((source_of == order[0]) | (taker == order[0]) | (sizes[taker] == 0), 0, jnp.maximum(slack, 0))
    passed = jax.random.randint(jax.random.fold_in(own, 4), (number_of // 2,), 0, 1 << 20) % (slack + 1)
    sizes = sizes.at[source_of].add(-passed).at[taker].add(passed)
    labels = jnp.searchsorted(jnp.cumsum(sizes), jnp.arange(rows * top), side="right").astype(jnp.int32)
    table = labels.reshape(top, rows).T
    table = table[jax.random.permutation(jax.random.fold_in(own, 1), rows)]
    rotation = jax.random.randint(jax.random.fold_in(own, 2), (rows, 1), 0, top)
    return jnp.take_along_axis(table, (jnp.arange(top)[None, :] + rotation) % top, axis=1)


def shares(count, total, most, lean, full):
    weights = [(1 << 20) // math.isqrt(rank ** lean) + 1 for rank in range(1, count + 1)]
    largest = most if full else min(most, max(-(-total // count), total * weights[0] // sum(weights)))
    least = 1 if total - largest >= count - 1 else 0
    given, rest = [largest] + [least] * (count - 1), total - largest - least * (count - 1)
    while rest > 0:
        candidates = [i for i in range(1, count) if given[i] < largest] or [i for i in range(1, count) if given[i] < most]
        whole, left = sum([weights[i] for i in candidates]), rest
        for i in candidates:
            extra = min(most - given[i], max(1, left * weights[i] // whole), rest)
            given[i] = given[i] + extra
            rest = rest - extra
    return np.array(given)


def noise(stream_key, extent, scale, limit, cuts=(), held_as=jnp.bfloat16):
    values = scale * jax.random.normal(stream_key, extent, jnp.float32)
    if cuts:
        values = values * block_levels(stream_key, extent, cuts, -0.22, 0.18)
    return jnp.clip(values, -limit, limit).astype(held_as)


def setup_inputs(seed: int = 0) -> dict:
    key_list = jax.random.split(jax.random.key(seed), 10)
    thickness = noise(key_list[0], (ELEMS,), 4.0, 24.0, ((0, 128),), jnp.float32)
    tile_weights = noise(key_list[1], (TILES, 128, 128), 128 ** -0.5, 0.5, ((0, 128),), jnp.float32)
    tile_dest_keys = jax.random.split(jax.random.fold_in(key_list[2], 1), TILES // TILES_DEV)
    tile_dest_turns = jax.random.permutation(jax.random.fold_in(key_list[2], 3), TILES // TILES_DEV)
    tile_dest = jax.vmap(lambda own, number: shared_out(jax.random.fold_in(key_list[2], 2), own, number, TILES_DEV, DEVICES, 1, CAP, 2))(tile_dest_keys, tile_dest_turns).reshape((TILES, 1))
    tile_row = place_ends(jax.random.randint(key_list[3], (TILES,), 0, LAT_DEV), jax.random.fold_in(key_list[3], 1), 0, LAT_DEV - 1).astype(jnp.int32)
    tile_col = place_ends(jax.random.randint(key_list[4], (TILES,), 0, NLON // 128), jax.random.fold_in(key_list[4], 1), 0, (NLON // 128) - 1).astype(jnp.int32)
    window = draw_window(jax.random.fold_in(key_list[9], 71), 0)
    quad_weights = jnp.clip(jnp.exp(math.log(2.0) - 1.3862944 * jax.random.uniform(key_list[6], (NLAT,), jnp.float32) ** block_levels(key_list[6], (NLAT,), ((0, 8),), -0.2, 0.2)), 0.5, 2.0)
    legendre = noise(key_list[7], (ORDERS, NLAT, LDEG), NLAT ** -0.5, 0.09375, ((0, 16), (1, 8)), jnp.float32)
    love_code = place_ends(jax.random.randint(key_list[8], (LDEG,), 100, 2001), jax.random.fold_in(key_list[8], 1), 100, 2000).astype(jnp.int32)
    return dict(thickness=thickness, tile_weights=tile_weights, tile_dest=tile_dest, tile_row=tile_row, tile_col=tile_col, window=window, quad_weights=quad_weights, legendre=legendre, love_code=love_code)


def make_table(window, count):
    column = jnp.arange(count, dtype=jnp.int32)
    phase = (column[:, None] * window[None, :].astype(jnp.int32)) % count
    angle = phase.astype(jnp.float32) * (2.0 * math.pi / count)
    return jnp.concatenate([jnp.cos(angle), jnp.sin(angle)], axis=1)


def reference(thickness, tile_weights, tile_dest, tile_row, tile_col, window, quad_weights, legendre, love_code):
    upper_limit = lax.Precision.HIGHEST
    blocks_per_row = NLON // 128
    elements = thickness.reshape(TILES, 128)
    cells = jnp.einsum("tce,te->tc", tile_weights, elements, precision=upper_limit)
    target = (tile_dest[:, 0] * LAT_DEV + tile_row) * blocks_per_row + tile_col
    grid = jnp.zeros((NLAT * blocks_per_row, 128), jnp.float32).at[target].add(cells)
    grid = grid.reshape(NLAT, NLON)
    table = make_table(window, NLON)
    spectra = jnp.dot(grid, table, precision=upper_limit) * (NLON ** -0.5)
    weight_applied = (spectra * quad_weights[:, None]).reshape(NLAT, 2, ORDERS)
    love = love_code.astype(jnp.float32) / 1000.0
    running_sum = jnp.einsum("qek,kqd->ked", weight_applied, legendre, precision=upper_limit)
    coefficients = running_sum * love[None, None, :]
    field_arrays = jnp.einsum("shq,saq->has", legendre, coefficients, precision=upper_limit)
    field_arrays = field_arrays.reshape(NLAT, 2 * ORDERS)
    response = jnp.dot(field_arrays, table.T, precision=upper_limit) * ((2 * ORDERS) ** -0.5)
    picked = response.reshape(NLAT * blocks_per_row, 128)[target]
    uplift = jnp.einsum("tce,tc->te", tile_weights, picked, precision=upper_limit).reshape(ELEMS)
    return uplift, coefficients
```

```python
import math

import jax
import jax.numpy as jnp
from jax import lax
from jax.experimental import pallas as pl
from jax.experimental.pallas import tpu as pltpu
from jax.sharding import PartitionSpec as P

NLON = 8192
F32 = jnp.float32
BF16 = jnp.bfloat16
MESH = pl.DeviceIdType.MESH
HIGHEST = lax.Precision.HIGHEST
NN = (((1,), (0,)), ((), ()))
NT = (((1,), (1,)), ((), ()))

BANDS = 8
ORDERS = 16
DEVICES = BANDS * ORDERS
TILES = 128
DEGREES = 4096
LAT_BAND = 512
LAT_DEV = 32
W_CHUNKS = 4
L_CHUNKS = 4
X_CHUNKS = 4
X_COLS = DEGREES // X_CHUNKS


def ring(k):
    return min(k, 4 - k)


OFFSETS = sorted(
    [
        (dy, dc, dz, dx)
        for dy in range(4)
        for dc in range(2)
        for dz in range(4)
        for dx in range(4)
        if (dy, dc, dz, dx) != (0, 0, 0, 0)
    ],
    key=lambda o: -(ring(o[0]) + ring(o[2]) + ring(o[3]) + 0.3 * o[1]),
)
BAND_OFFSETS = sorted(
    [(dy, dc) for dy in range(4) for dc in range(2) if (dy, dc) != (0, 0)],
    key=lambda o: -(ring(o[0]) + 0.3 * o[1]),
)


def dot(a, b, dims):
    return lax.dot_general(a, b, dims, preferred_element_type=F32)


def split(x):
    high = x.astype(BF16)
    low = (x - high.astype(F32)).astype(BF16)
    return high, low


def iota(shape, dim):
    return lax.broadcasted_iota(jnp.int32, shape, dim)


def body(
    thick_any,
    weights_any,
    dest_any,
    row_any,
    col_any,
    window_any,
    quad_any,
    legendre_any,
    love_any,
    uplift_ref,
    coef_ref,
    thick,
    dest,
    row,
    col,
    window,
    quad,
    love,
    w_f32,
    w_hi,
    w_lo,
    l_f32,
    l_hi,
    l_lo,
    cells,
    send_a,
    recv_a,
    shares,
    send_b,
    recv_b,
    spread,
    mask,
    pick,
    small_sem,
    w_sem,
    l_sem,
    a_send,
    a_recv,
    x_send,
    x_recv,
    b_send,
    b_recv,
):
    band = lax.axis_index("band")
    order = lax.axis_index("order")
    me = band * ORDERS + order
    y, core, z, x = band // 2, band % 2, order // 4, order % 4
    band_of = {(i, j): ((y + i) % 4) * 2 + (core + j) % 2 for i in range(4) for j in range(2)}
    order_of = {(i, j): ((z + i) % 4) * 4 + (x + j) % 4 for i in range(4) for j in range(4)}
    peers = [(band_of[dy, dc], order_of[dz, dx]) for dy, dc, dz, dx in OFFSETS]

    rows_w = TILES // W_CHUNKS
    rows_l = LAT_BAND // L_CHUNKS
    small = []
    for i, (source, target) in enumerate(
        (
            (thick_any, thick),
            (dest_any, dest),
            (row_any, row),
            (col_any, col),
            (window_any, window),
            (quad_any, quad),
            (love_any, love),
        )
    ):
        small.append(pltpu.make_async_copy(source, target, small_sem.at[i]))
        small[-1].start()
    w_copies, l_copies = [], []
    for i in range(W_CHUNKS):
        at = pl.ds(i * rows_w, rows_w)
        w_copies.append(pltpu.make_async_copy(weights_any.at[at], w_f32.at[at], w_sem.at[i]))
        w_copies[-1].start()
    for i in range(L_CHUNKS):
        at = pl.ds(i * rows_l, rows_l)
        l_copies.append(pltpu.make_async_copy(legendre_any.at[0, at], l_f32.at[at], l_sem.at[i]))
        l_copies[-1].start()

    barrier = pltpu.get_barrier_semaphore()
    for ids in peers:
        pl.semaphore_signal(barrier, inc=1, device_id=ids, device_id_type=MESH)

    for copy in small:
        copy.wait()

    own_lane = iota((8, 1024), 1) // 128 == iota((8, 1024), 0)

    def cells_of(group, _):
        tiles = pl.ds(pl.multiple_of(group * 8, 8), 8)
        high, low = split(w_f32[tiles])
        flat = pl.ds(pl.multiple_of(group * 1024, 1024), 1024)
        w_hi[flat] = high.reshape(1024, 128)
        w_lo[flat] = low.reshape(1024, 128)
        values = thick[tiles]
        values = jnp.where(own_lane, jnp.concatenate([values] * 8, axis=1), 0.0)
        v_high, v_low = split(values)
        left = jnp.concatenate([v_high, v_low], axis=0)
        right = jnp.concatenate([high[i] for i in range(8)], axis=1)
        both = dot(left, right, NT)
        right = jnp.concatenate([low[i] for i in range(8)], axis=1)
        cells[tiles] = both[0:8] + both[8:16] + dot(v_high, right, NT)
        return 0

    for i in range(W_CHUNKS):
        w_copies[i].wait()
        lax.fori_loop(i * rows_w // 8, (i + 1) * rows_w // 8, cells_of, 0)

    lane = iota((ORDERS, 128), 1)
    orders = jnp.zeros((ORDERS, 128), jnp.int32)
    for i in range(ORDERS):
        orders = jnp.where(iota((ORDERS, 128), 0) == i, window[i], orders)
    angle = ((orders * lane) & (NLON - 1)).astype(F32) * (2.0 * math.pi / NLON)
    table = jnp.concatenate([jnp.cos(angle), jnp.sin(angle)], axis=0)
    turn = ((orders * col[...]) & 63).astype(F32) * (2.0 * math.pi / 64)
    turn_cos, turn_sin = jnp.cos(turn), jnp.sin(turn)

    raw = lax.dot_general(table, cells[...], NT, precision=HIGHEST, preferred_element_type=F32)
    scale = NLON ** (-0.5)
    part_cos = (raw[0:16] * turn_cos - raw[16:32] * turn_sin) * scale
    part_sin = (raw[16:32] * turn_cos + raw[0:16] * turn_sin) * scale

    owner = jnp.broadcast_to(dest[...], (TILES, TILES))
    earlier = (owner.T == owner) & (iota((TILES, TILES), 0) < iota((TILES, TILES), 1))
    slot = jnp.sum(jnp.where(earlier, 1.0, 0.0), axis=0, keepdims=True).astype(jnp.int32)
    place = slot * 16 + (dest[...] & 15)
    tile_band = dest[...] >> 4
    at_place = jnp.where(iota((256, TILES), 0) == tile_band * 32 + place, 1.0, 0.0).astype(BF16)
    code = jnp.broadcast_to((row[...] + 1).astype(F32), (ORDERS, TILES)).astype(BF16)
    high, low = split(jnp.concatenate([part_cos, part_sin], axis=0))
    packed = dot(jnp.concatenate([high, low, code], axis=0), at_place, NT)
    values = packed[0:32] + packed[32:64]
    codes = packed[64:80]
    zeros = jnp.zeros((ORDERS, 32), F32)
    for i in range(BANDS):
        cut = slice(32 * i, 32 * i + 32)
        send_a[ORDERS * i : ORDERS * (i + 1)] = jnp.concatenate(
            [values[0:16, cut], values[16:32, cut], codes[:, cut], zeros], axis=1
        )

    def split_rows(step, _):
        at = pl.ds(pl.multiple_of(step * 16, 16), 16)
        high, low = split(l_f32[at])
        l_hi[at] = high
        l_lo[at] = low
        return 0

    for i in range(L_CHUNKS):
        l_copies[i].wait()
        lax.fori_loop(i * rows_l // 16, (i + 1) * rows_l // 16, split_rows, 0)

    pl.semaphore_wait(barrier, DEVICES - 1)

    def to_all(source, target, send_sem, recv_sem):
        for peer_band, peer_order in peers:
            peer = peer_band * ORDERS + peer_order
            pltpu.make_async_remote_copy(
                src_ref=source.at[pl.ds(peer, 1)],
                dst_ref=target.at[pl.ds(me, 1)],
                send_sem=send_sem.at[0],
                recv_sem=recv_sem.at[0],
                device_id=(peer_band, peer_order),
                device_id_type=MESH,
            ).start()
        target[pl.ds(me, 1)] = source[pl.ds(me, 1)]

    def wait_all(ref, sem):
        others = ref.at[pl.ds(0, DEVICES - 1)]
        pltpu.make_async_copy(others, others, sem.at[0]).wait()

    to_all(send_a, recv_a, a_send, a_recv)

    group = iota((128, 1024), 1) // 32
    spread[...] = jnp.where(iota((128, 1024), 0) == 64 + group, 1.0, 0.0).astype(BF16)
    spot = iota((128, TILES), 0) & 63
    for i in range(BANDS):
        mine = tile_band == i
        for p in range(2):
            pick[128 * i : 128 * (i + 1), 128 * p : 128 * (p + 1)] = jnp.where(
                mine & (spot == p * 32 + place), 1.0, 0.0
            ).astype(BF16)
    factor = love[...].astype(F32) / 1000.0

    wait_all(recv_a, a_recv)

    got = recv_a[...]
    code = dot(got.astype(BF16), spread[...], NN)
    wanted = ((iota((128, 1024), 1) & 31) + 1).astype(F32)
    chosen = jnp.where(code == wanted, 1.0, 0.0).astype(BF16)
    mask[...] = chosen
    high, low = split(got.T[0:64])
    sums = dot(jnp.concatenate([high, low], axis=0), chosen, NN)
    sums = sums[0:64] + sums[64:128]
    diagonal = iota((64, 1024), 0) & 31
    sums = jnp.where(diagonal == iota((64, 1024), 1) // 32, sums, 0.0)
    spectra = jnp.concatenate(
        [
            jnp.sum(sums[0:32], axis=0, keepdims=True),
            jnp.sum(sums[32:64], axis=0, keepdims=True),
        ],
        axis=0,
    )
    spectra = (spectra[:, 0:512] + spectra[:, 512:1024]) * quad[...]

    high, low = split(spectra)
    both = jnp.concatenate([high.astype(F32), low.astype(F32)], axis=0).astype(BF16)
    copies = []
    for k in range(X_CHUNKS):
        cut = pl.ds(k * X_COLS, X_COLS)
        share = dot(both, l_hi[:, cut], NN)
        share = share[0:2] + share[2:4] + dot(high, l_lo[:, cut], NN)
        shares[k, band] = share
        for dy, dc in BAND_OFFSETS:
            copy = pltpu.make_async_remote_copy(
                src_ref=shares.at[k, band],
                dst_ref=shares.at[k, band],
                send_sem=x_send.at[k],
                recv_sem=x_recv.at[k],
                device_id=(band_of[dy, dc], order),
                device_id_type=MESH,
            )
            copy.start()

    fields = jnp.zeros((2, LAT_BAND), F32)
    for k in range(X_CHUNKS):
        cut = pl.ds(k * X_COLS, X_COLS)
        others = shares.at[k, pl.ds(0, BANDS - 1)]
        pltpu.make_async_copy(others, others, x_recv.at[k]).wait()
        total = shares[k, 0]
        for i in range(1, BANDS):
            total = total + shares[k, i]
        total = total * factor[:, k * X_COLS : (k + 1) * X_COLS]
        coef_ref[0, :, cut] = total
        high, low = split(total)
        both = jnp.concatenate([high.astype(F32), low.astype(F32)], axis=0).astype(BF16)
        term = dot(both, l_hi[:, cut], NT)
        fields = fields + (term[0:2] + term[2:4] + dot(high, l_lo[:, cut], NT))

    twice = jnp.concatenate([fields, fields], axis=1)
    twice = jnp.concatenate(
        [
            jnp.broadcast_to(twice[0:1], (32, 1024)),
            jnp.broadcast_to(twice[1:2], (32, 1024)),
        ],
        axis=0,
    )
    twice = jnp.where(diagonal == iota((64, 1024), 1) // 32, twice, 0.0)
    high, low = split(twice)
    send_b[...] = dot(mask[...], jnp.concatenate([high, low], axis=0), NT)
    to_all(send_b, recv_b, b_send, b_recv)
    for k in range(X_CHUNKS):
        others = shares.at[k, pl.ds(0, BANDS - 1)]
        pltpu.make_async_copy(others, others, x_send.at[k]).wait()
    wait_all(send_a, a_send)
    wait_all(recv_b, b_recv)

    back = recv_b[...].astype(BF16)
    back = jnp.concatenate([back[16 * i : 16 * (i + 1)] for i in range(BANDS)], axis=1)
    tile_fields = dot(back, pick[...], NN)
    f_cos, f_sin = tile_fields[:, 0:128], tile_fields[:, 128:256]
    scale = (2 * ORDERS) ** (-0.5)
    turned = jnp.concatenate(
        [
            (f_cos * turn_cos + f_sin * turn_sin) * scale,
            (f_sin * turn_cos - f_cos * turn_sin) * scale,
        ],
        axis=0,
    )
    response = lax.dot_general(
        turned.T, table, NN, precision=HIGHEST, preferred_element_type=F32
    )
    for g in range(TILES // 8):
        values = response[8 * g : 8 * (g + 1)]
        values = jnp.where(own_lane, jnp.concatenate([values] * 8, axis=1), 0.0)
        v_high, v_low = split(values)
        flat = pl.ds(1024 * g, 1024)
        both = dot(jnp.concatenate([v_high, v_low], axis=0), w_hi[flat], NN)
        uplift_ref[8 * g : 8 * (g + 1)] = both[0:8] + both[8:16] + dot(v_high, w_lo[flat], NN)
    wait_all(send_b, b_send)


def on_device(
    thickness,
    tile_weights,
    tile_dest,
    tile_row,
    tile_col,
    window,
    quad_weights,
    legendre,
    love_code,
):
    anywhere = pl.BlockSpec(memory_space=pl.ANY)
    vmem = pl.BlockSpec(memory_space=pltpu.VMEM)
    uplift, coefficients = pl.pallas_call(
        body,
        out_shape=(
            jax.ShapeDtypeStruct((TILES, 128), F32),
            jax.ShapeDtypeStruct((1, 2, DEGREES), F32),
        ),
        in_specs=[anywhere] * 9,
        out_specs=(vmem, vmem),
        scratch_shapes=[
            pltpu.VMEM((TILES, 128), F32),
            pltpu.VMEM((1, TILES), jnp.int32),
            pltpu.VMEM((1, TILES), jnp.int32),
            pltpu.VMEM((1, TILES), jnp.int32),
            pltpu.SMEM((ORDERS,), jnp.int32),
            pltpu.VMEM((1, LAT_BAND), F32),
            pltpu.VMEM((1, DEGREES), jnp.int32),
            pltpu.VMEM((TILES, 128, 128), F32),
            pltpu.VMEM((TILES * 128, 128), BF16),
            pltpu.VMEM((TILES * 128, 128), BF16),
            pltpu.VMEM((LAT_BAND, DEGREES), F32),
            pltpu.VMEM((LAT_BAND, DEGREES), BF16),
            pltpu.VMEM((LAT_BAND, DEGREES), BF16),
            pltpu.VMEM((TILES, 128), F32),
            pltpu.VMEM((DEVICES, 128), F32),
            pltpu.VMEM((DEVICES, 128), F32),
            pltpu.VMEM((X_CHUNKS, BANDS, 2, X_COLS), F32),
            pltpu.VMEM((DEVICES, 128), F32),
            pltpu.VMEM((DEVICES, 128), F32),
            pltpu.VMEM((128, 1024), BF16),
            pltpu.VMEM((128, 1024), BF16),
            pltpu.VMEM((1024, 256), BF16),
            pltpu.SemaphoreType.DMA((7,)),
            pltpu.SemaphoreType.DMA((W_CHUNKS,)),
            pltpu.SemaphoreType.DMA((L_CHUNKS,)),
            pltpu.SemaphoreType.DMA((1,)),
            pltpu.SemaphoreType.DMA((1,)),
            pltpu.SemaphoreType.DMA((X_CHUNKS,)),
            pltpu.SemaphoreType.DMA((X_CHUNKS,)),
            pltpu.SemaphoreType.DMA((1,)),
            pltpu.SemaphoreType.DMA((1,)),
        ],
        compiler_params=pltpu.CompilerParams(
            collective_id=0, has_side_effects=True, vmem_limit_bytes=52 * 1024 * 1024
        ),
    )(
        thickness.reshape(TILES, 128),
        tile_weights,
        tile_dest.reshape(1, TILES),
        tile_row.reshape(1, TILES),
        tile_col.reshape(1, TILES),
        window,
        quad_weights.reshape(1, LAT_BAND),
        legendre,
        love_code.reshape(1, DEGREES),
    )
    return uplift.reshape(TILES * 128), coefficients


def solution(mesh):
    return jax.shard_map(
        on_device,
        mesh=mesh,
        in_specs=(
            P(("band", "order")),
            P(("band", "order"), None, None),
            P(("band", "order"), None),
            P(("band", "order")),
            P(("band", "order")),
            P(),
            P("band"),
            P("order", "band", None),
            P(),
        ),
        out_specs=(P(("band", "order")), P("order", None, None)),
        check_vma=False,
    )
```

```python
import math

import jax
import jax.numpy as jnp
from jax import lax
from jax.experimental import pallas as pl
from jax.experimental.pallas import tpu as pltpu
from jax.sharding import PartitionSpec as P

NLON = 8192
F32 = jnp.float32
BF16 = jnp.bfloat16
MESH = pl.DeviceIdType.MESH
HIGHEST = lax.Precision.HIGHEST
NN = (((1,), (0,)), ((), ()))
NT = (((1,), (1,)), ((), ()))

BANDS = 8
ORDERS = 16
DEVICES = BANDS * ORDERS
TILES = 128
DEGREES = 4096
LAT_BAND = 512
LAT_DEV = 32
W_CHUNKS = 2
GROUP = 16
L_CHUNKS = 4
X_CHUNKS = 4
X_COLS = DEGREES // X_CHUNKS


def ring(k):
    return min(k, 4 - k)


OFFSETS = sorted(
    [
        (dy, dc, dz, dx)
        for dy in range(4)
        for dc in range(2)
        for dz in range(4)
        for dx in range(4)
        if (dy, dc, dz, dx) != (0, 0, 0, 0)
    ],
    key=lambda o: -(ring(o[0]) + ring(o[2]) + ring(o[3]) + 0.3 * o[1]),
)
BAND_OFFSETS = sorted(
    [(dy, dc) for dy in range(4) for dc in range(2) if (dy, dc) != (0, 0)],
    key=lambda o: -(ring(o[0]) + 0.3 * o[1]),
)


def dot(a, b, dims):
    return lax.dot_general(a, b, dims, preferred_element_type=F32)


def split(x):
    high = x.astype(BF16)
    low = (x - high.astype(F32)).astype(BF16)
    return high, low


def iota(shape, dim):
    return lax.broadcasted_iota(jnp.int32, shape, dim)


def body(
    thick_any,
    weights_any,
    dest_any,
    row_any,
    col_any,
    window_any,
    quad_any,
    legendre_any,
    love_any,
    uplift_ref,
    coef_ref,
    thick,
    dest,
    row,
    col,
    window,
    quad,
    love,
    w_f32,
    w_hi,
    w_lo,
    l_f32,
    l_hi,
    l_lo,
    cells,
    send_a,
    recv_a,
    shares,
    send_b,
    recv_b,
    spread,
    mask,
    pick,
    small_sem,
    w_sem,
    l_sem,
    a_send,
    a_recv,
    x_send,
    x_recv,
    b_send,
    b_recv,
):
    band = lax.axis_index("band")
    order = lax.axis_index("order")
    me = band * ORDERS + order
    y, core, z, x = band // 2, band % 2, order // 4, order % 4
    band_of = {(i, j): ((y + i) % 4) * 2 + (core + j) % 2 for i in range(4) for j in range(2)}
    order_of = {(i, j): ((z + i) % 4) * 4 + (x + j) % 4 for i in range(4) for j in range(4)}
    peers = [(band_of[dy, dc], order_of[dz, dx]) for dy, dc, dz, dx in OFFSETS]

    rows_w = TILES // W_CHUNKS
    rows_l = LAT_BAND // L_CHUNKS
    small = []
    for i, (source, target) in enumerate(
        (
            (thick_any, thick),
            (dest_any, dest),
            (row_any, row),
            (col_any, col),
            (window_any, window),
            (quad_any, quad),
            (love_any, love),
        )
    ):
        small.append(pltpu.make_async_copy(source, target, small_sem.at[i]))
        small[-1].start()
    w_copies, l_copies = [], []
    for i in range(W_CHUNKS):
        at = pl.ds(i * rows_w, rows_w)
        w_copies.append(pltpu.make_async_copy(weights_any.at[at], w_f32.at[at], w_sem.at[i]))
        w_copies[-1].start()
    for i in range(L_CHUNKS):
        at = pl.ds(i * rows_l, rows_l)
        l_copies.append(pltpu.make_async_copy(legendre_any.at[0, at], l_f32.at[at], l_sem.at[i]))

    barrier = pltpu.get_barrier_semaphore()
    for ids in peers:
        pl.semaphore_signal(barrier, inc=1, device_id=ids, device_id_type=MESH)

    for copy in small:
        copy.wait()

    lane = iota((ORDERS, 128), 1)
    orders = jnp.zeros((ORDERS, 128), jnp.int32)
    for i in range(ORDERS):
        orders = jnp.where(iota((ORDERS, 128), 0) == i, window[i], orders)
    angle = ((orders * lane) & (NLON - 1)).astype(F32) * (2.0 * math.pi / NLON)
    table = jnp.concatenate([jnp.cos(angle), jnp.sin(angle)], axis=0)
    turn = ((orders * col[...]) & 63).astype(F32) * (2.0 * math.pi / 64)
    turn_cos, turn_sin = jnp.cos(turn), jnp.sin(turn)

    owner = jnp.broadcast_to(dest[...], (TILES, TILES))
    earlier = (owner.T == owner) & (iota((TILES, TILES), 0) < iota((TILES, TILES), 1))
    slot = jnp.sum(jnp.where(earlier, 1.0, 0.0), axis=0, keepdims=True).astype(jnp.int32)
    place = slot * 16 + (dest[...] & 15)
    tile_band = dest[...] >> 4
    at_place = jnp.where(iota((256, TILES), 0) == tile_band * 32 + place, 1.0, 0.0).astype(BF16)
    code = jnp.broadcast_to((row[...] + 1).astype(F32), (ORDERS, TILES)).astype(BF16)
    own_lane = iota((GROUP, 128 * GROUP), 1) // 128 == iota((GROUP, 128 * GROUP), 0)

    def cells_of(i, _):
        tiles = pl.ds(pl.multiple_of(i * GROUP, 8), GROUP)
        values = thick[tiles]
        values = jnp.where(own_lane, jnp.concatenate([values] * GROUP, axis=1), 0.0)
        v_high, v_low = split(values)
        pieces = [split(w_f32[i * GROUP + t]) for t in range(GROUP)]
        right = jnp.concatenate([high for high, _ in pieces], axis=1)
        both = dot(jnp.concatenate([v_high, v_low], axis=0), right, NT)
        right = jnp.concatenate([low for _, low in pieces], axis=1)
        cells[tiles] = both[0:GROUP] + both[GROUP:] + dot(v_high, right, NT)
        return 0

    for i in range(W_CHUNKS):
        w_copies[i].wait()
        if i == 0:
            for copy in l_copies:
                copy.start()
        n = rows_w // GROUP
        lax.fori_loop(i * n, (i + 1) * n, cells_of, 0, unroll=2)

    raw = lax.dot_general(table, cells[...], NT, precision=HIGHEST, preferred_element_type=F32)
    scale = NLON ** (-0.5)
    part_cos = (raw[0:16] * turn_cos - raw[16:32] * turn_sin) * scale
    part_sin = (raw[16:32] * turn_cos + raw[0:16] * turn_sin) * scale

    high, low = split(jnp.concatenate([part_cos, part_sin], axis=0))
    packed = dot(jnp.concatenate([high, low, code], axis=0), at_place, NT)
    values = packed[0:32] + packed[32:64]
    codes = packed[64:80]
    zeros = jnp.zeros((ORDERS, 32), F32)
    for i in range(BANDS):
        cut = slice(32 * i, 32 * i + 32)
        send_a[ORDERS * i : ORDERS * (i + 1)] = jnp.concatenate(
            [values[0:16, cut], values[16:32, cut], codes[:, cut], zeros], axis=1
        )

    pl.semaphore_wait(barrier, DEVICES - 1)

    def to_all(source, target, send_sem, recv_sem):
        for peer_band, peer_order in peers:
            peer = peer_band * ORDERS + peer_order
            pltpu.make_async_remote_copy(
                src_ref=source.at[pl.ds(peer, 1)],
                dst_ref=target.at[pl.ds(me, 1)],
                send_sem=send_sem.at[0],
                recv_sem=recv_sem.at[0],
                device_id=(peer_band, peer_order),
                device_id_type=MESH,
            ).start()
        target[pl.ds(me, 1)] = source[pl.ds(me, 1)]

    def wait_all(ref, sem):
        others = ref.at[pl.ds(0, DEVICES - 1)]
        pltpu.make_async_copy(others, others, sem.at[0]).wait()

    to_all(send_a, recv_a, a_send, a_recv)

    group = iota((128, 1024), 1) // 32
    spread[...] = jnp.where(iota((128, 1024), 0) == 64 + group, 1.0, 0.0).astype(BF16)
    spot = iota((128, TILES), 0) & 63
    for i in range(BANDS):
        mine = tile_band == i
        for p in range(2):
            pick[128 * i : 128 * (i + 1), 128 * p : 128 * (p + 1)] = jnp.where(
                mine & (spot == p * 32 + place), 1.0, 0.0
            ).astype(BF16)
    factor = love[...].astype(F32) / 1000.0

    def split_tiles(step, _):
        at = pl.ds(pl.multiple_of(step * 4, 4), 4)
        flat = pl.ds(pl.multiple_of(step * 512, 512), 512)
        high, low = split(w_f32[at].reshape(512, 128))
        w_hi[flat] = high
        w_lo[flat] = low
        return 0

    lax.fori_loop(0, TILES // 4, split_tiles, 0)

    def split_rows(step, _):
        at = pl.ds(pl.multiple_of(step * 16, 16), 16)
        high, low = split(l_f32[at])
        l_hi[at] = high
        l_lo[at] = low
        return 0

    for i in range(L_CHUNKS):
        l_copies[i].wait()
        lax.fori_loop(i * rows_l // 16, (i + 1) * rows_l // 16, split_rows, 0)

    wait_all(recv_a, a_recv)

    got = recv_a[...]
    code = dot(got.astype(BF16), spread[...], NN)
    wanted = ((iota((128, 1024), 1) & 31) + 1).astype(F32)
    chosen = jnp.where(code == wanted, 1.0, 0.0).astype(BF16)
    mask[...] = chosen
    high, low = split(got.T[0:64])
    sums = dot(jnp.concatenate([high, low], axis=0), chosen, NN)
    sums = sums[0:64] + sums[64:128]
    diagonal = iota((64, 1024), 0) & 31
    sums = jnp.where(diagonal == iota((64, 1024), 1) // 32, sums, 0.0)
    spectra = jnp.concatenate(
        [
            jnp.sum(sums[0:32], axis=0, keepdims=True),
            jnp.sum(sums[32:64], axis=0, keepdims=True),
        ],
        axis=0,
    )
    spectra = (spectra[:, 0:512] + spectra[:, 512:1024]) * quad[...]

    high, low = split(spectra)
    both = jnp.concatenate([high.astype(F32), low.astype(F32)], axis=0).astype(BF16)
    copies = []
    for k in range(X_CHUNKS):
        cut = pl.ds(k * X_COLS, X_COLS)
        share = dot(both, l_hi[:, cut], NN)
        share = share[0:2] + share[2:4] + dot(high, l_lo[:, cut], NN)
        shares[k, band] = share
        for dy, dc in BAND_OFFSETS:
            copy = pltpu.make_async_remote_copy(
                src_ref=shares.at[k, band],
                dst_ref=shares.at[k, band],
                send_sem=x_send.at[k],
                recv_sem=x_recv.at[k],
                device_id=(band_of[dy, dc], order),
                device_id_type=MESH,
            )
            copy.start()

    fields = jnp.zeros((2, LAT_BAND), F32)
    for k in range(X_CHUNKS):
        cut = pl.ds(k * X_COLS, X_COLS)
        others = shares.at[k, pl.ds(0, BANDS - 1)]
        pltpu.make_async_copy(others, others, x_recv.at[k]).wait()
        total = shares[k, 0]
        for i in range(1, BANDS):
            total = total + shares[k, i]
        total = total * factor[:, k * X_COLS : (k + 1) * X_COLS]
        coef_ref[0, :, cut] = total
        high, low = split(total)
        both = jnp.concatenate([high.astype(F32), low.astype(F32)], axis=0).astype(BF16)
        term = dot(both, l_hi[:, cut], NT)
        fields = fields + (term[0:2] + term[2:4] + dot(high, l_lo[:, cut], NT))

    twice = jnp.concatenate([fields, fields], axis=1)
    twice = jnp.concatenate(
        [
            jnp.broadcast_to(twice[0:1], (32, 1024)),
            jnp.broadcast_to(twice[1:2], (32, 1024)),
        ],
        axis=0,
    )
    twice = jnp.where(diagonal == iota((64, 1024), 1) // 32, twice, 0.0)
    high, low = split(twice)
    send_b[...] = dot(mask[...], jnp.concatenate([high, low], axis=0), NT)
    to_all(send_b, recv_b, b_send, b_recv)
    for k in range(X_CHUNKS):
        others = shares.at[k, pl.ds(0, BANDS - 1)]
        pltpu.make_async_copy(others, others, x_send.at[k]).wait()
    wait_all(send_a, a_send)
    wait_all(recv_b, b_recv)

    back = recv_b[...].astype(BF16)
    back = jnp.concatenate([back[16 * i : 16 * (i + 1)] for i in range(BANDS)], axis=1)
    tile_fields = dot(back, pick[...], NN)
    f_cos, f_sin = tile_fields[:, 0:128], tile_fields[:, 128:256]
    scale = (2 * ORDERS) ** (-0.5)
    turned = jnp.concatenate(
        [
            (f_cos * turn_cos + f_sin * turn_sin) * scale,
            (f_sin * turn_cos - f_cos * turn_sin) * scale,
        ],
        axis=0,
    )
    response = lax.dot_general(
        turned.T, table, NN, precision=HIGHEST, preferred_element_type=F32
    )
    own_lane = iota((8, 1024), 1) // 128 == iota((8, 1024), 0)
    for g in range(TILES // 8):
        values = response[8 * g : 8 * (g + 1)]
        values = jnp.where(own_lane, jnp.concatenate([values] * 8, axis=1), 0.0)
        v_high, v_low = split(values)
        flat = pl.ds(1024 * g, 1024)
        both = dot(jnp.concatenate([v_high, v_low], axis=0), w_hi[flat], NN)
        uplift_ref[8 * g : 8 * (g + 1)] = both[0:8] + both[8:16] + dot(v_high, w_lo[flat], NN)
    wait_all(send_b, b_send)


def hand_over(uplift_in, coef_in, uplift_out, coef_out):
    uplift_out[...] = uplift_in[...]
    coef_out[...] = coef_in[...]


def on_device(
    thickness,
    tile_weights,
    tile_dest,
    tile_row,
    tile_col,
    window,
    quad_weights,
    legendre,
    love_code,
):
    hbm = pl.BlockSpec(memory_space=pltpu.HBM)
    vmem = pl.BlockSpec(memory_space=pltpu.VMEM)
    uplift, coefficients = pl.pallas_call(
        body,
        out_shape=(
            jax.ShapeDtypeStruct((TILES, 128), F32),
            jax.ShapeDtypeStruct((1, 2, DEGREES), F32),
        ),
        in_specs=[hbm] * 9,
        out_specs=(vmem, vmem),
        scratch_shapes=[
            pltpu.VMEM((TILES, 128), F32),
            pltpu.VMEM((1, TILES), jnp.int32),
            pltpu.VMEM((1, TILES), jnp.int32),
            pltpu.VMEM((1, TILES), jnp.int32),
            pltpu.SMEM((ORDERS,), jnp.int32),
            pltpu.VMEM((1, LAT_BAND), F32),
            pltpu.VMEM((1, DEGREES), jnp.int32),
            pltpu.VMEM((TILES, 128, 128), F32),
            pltpu.VMEM((TILES * 128, 128), BF16),
            pltpu.VMEM((TILES * 128, 128), BF16),
            pltpu.VMEM((LAT_BAND, DEGREES), F32),
            pltpu.VMEM((LAT_BAND, DEGREES), BF16),
            pltpu.VMEM((LAT_BAND, DEGREES), BF16),
            pltpu.VMEM((TILES, 128), F32),
            pltpu.VMEM((DEVICES, 128), F32),
            pltpu.VMEM((DEVICES, 128), F32),
            pltpu.VMEM((X_CHUNKS, BANDS, 2, X_COLS), F32),
            pltpu.VMEM((DEVICES, 128), F32),
            pltpu.VMEM((DEVICES, 128), F32),
            pltpu.VMEM((128, 1024), BF16),
            pltpu.VMEM((128, 1024), BF16),
            pltpu.VMEM((1024, 256), BF16),
            pltpu.SemaphoreType.DMA((7,)),
            pltpu.SemaphoreType.DMA((W_CHUNKS,)),
            pltpu.SemaphoreType.DMA((L_CHUNKS,)),
            pltpu.SemaphoreType.DMA((1,)),
            pltpu.SemaphoreType.DMA((1,)),
            pltpu.SemaphoreType.DMA((X_CHUNKS,)),
            pltpu.SemaphoreType.DMA((X_CHUNKS,)),
            pltpu.SemaphoreType.DMA((1,)),
            pltpu.SemaphoreType.DMA((1,)),
        ],
        compiler_params=pltpu.CompilerParams(
            collective_id=0, has_side_effects=True, vmem_limit_bytes=62 * 1024 * 1024
        ),
    )(
        thickness.reshape(TILES, 128),
        tile_weights,
        tile_dest.reshape(1, TILES),
        tile_row.reshape(1, TILES),
        tile_col.reshape(1, TILES),
        window,
        quad_weights.reshape(1, LAT_BAND),
        legendre,
        love_code.reshape(1, DEGREES),
    )
    uplift, coefficients = pl.pallas_call(
        hand_over,
        out_shape=(
            jax.ShapeDtypeStruct((TILES, 128), F32),
            jax.ShapeDtypeStruct((1, 2, DEGREES), F32),
        ),
        in_specs=[vmem, vmem],
        out_specs=(vmem, vmem),
        compiler_params=pltpu.CompilerParams(vmem_limit_bytes=62 * 1024 * 1024),
    )(uplift, coefficients)
    return uplift.reshape(TILES * 128), coefficients


def solution(mesh):
    return jax.shard_map(
        on_device,
        mesh=mesh,
        in_specs=(
            P(("band", "order")),
            P(("band", "order"), None, None),
            P(("band", "order"), None),
            P(("band", "order")),
            P(("band", "order")),
            P(),
            P("band"),
            P("order", "band", None),
            P(),
        ),
        out_specs=(P(("band", "order")), P("order", None, None)),
        check_vma=False,
    )
```

```python
import math

import jax
import jax.numpy as jnp
from jax import lax
from jax.experimental import pallas as pl
from jax.experimental.pallas import tpu as pltpu
from jax.sharding import PartitionSpec as P

NLON = 8192
F32 = jnp.float32
BF16 = jnp.bfloat16
MESH = pl.DeviceIdType.MESH
NN = (((1,), (0,)), ((), ()))
NT = (((1,), (1,)), ((), ()))

BANDS = 8
ORDERS = 16
DEVICES = BANDS * ORDERS
TILES = 128
DEGREES = 4096
LAT_BAND = 512
LAT_DEV = 32
W_CHUNKS = 4
GROUP = 16
L_CHUNKS = 4
X_CHUNKS = 4
X_COLS = DEGREES // X_CHUNKS


def ring(k):
    return min(k, 4 - k)


OFFSETS = sorted(
    [
        (dy, dc, dz, dx)
        for dy in range(4)
        for dc in range(2)
        for dz in range(4)
        for dx in range(4)
        if (dy, dc, dz, dx) != (0, 0, 0, 0)
    ],
    key=lambda o: -(ring(o[0]) + ring(o[2]) + ring(o[3]) + 0.3 * o[1]),
)
BAND_OFFSETS = sorted(
    [(dy, dc) for dy in range(4) for dc in range(2) if (dy, dc) != (0, 0)],
    key=lambda o: -(ring(o[0]) + 0.3 * o[1]),
)


def dot(a, b, dims):
    return lax.dot_general(a, b, dims, preferred_element_type=F32)


def split(x):
    high = x.astype(BF16)
    low = (x - high.astype(F32)).astype(BF16)
    return high, low


def iota(shape, dim):
    return lax.broadcasted_iota(jnp.int32, shape, dim)


def body(
    thick_any,
    weights_any,
    dest_any,
    row_any,
    col_any,
    window_any,
    quad_any,
    legendre_any,
    love_any,
    uplift_ref,
    coef_ref,
    thick,
    dest,
    row,
    col,
    window,
    quad,
    love,
    w_f32,
    w_hi,
    w_lo,
    l_f32,
    l_hi,
    l_lo,
    t_hi,
    t_lo,
    cells,
    send_a,
    recv_a,
    shares,
    send_b,
    recv_b,
    spread,
    mask,
    pick,
    small_sem,
    w_sem,
    l_sem,
    a_send,
    a_recv,
    x_send,
    x_recv,
    b_send,
    b_recv,
):
    band = lax.axis_index("band")
    order = lax.axis_index("order")
    me = band * ORDERS + order
    y, core, z, x = band // 2, band % 2, order // 4, order % 4
    band_of = {(i, j): ((y + i) % 4) * 2 + (core + j) % 2 for i in range(4) for j in range(2)}
    order_of = {(i, j): ((z + i) % 4) * 4 + (x + j) % 4 for i in range(4) for j in range(4)}
    peers = [(band_of[dy, dc], order_of[dz, dx]) for dy, dc, dz, dx in OFFSETS]

    rows_w = TILES // W_CHUNKS
    rows_l = LAT_BAND // L_CHUNKS
    small = []
    for i, (source, target) in enumerate(
        (
            (thick_any, thick),
            (dest_any, dest),
            (row_any, row),
            (col_any, col),
            (window_any, window),
            (quad_any, quad),
            (love_any, love),
        )
    ):
        small.append(pltpu.make_async_copy(source, target, small_sem.at[i]))
        small[-1].start()
    w_copies, l_copies = [], []
    for i in range(W_CHUNKS):
        at = pl.ds(i * rows_w, rows_w)
        w_copies.append(pltpu.make_async_copy(weights_any.at[at], w_f32.at[at], w_sem.at[i]))
        if i < W_CHUNKS // 2:
            w_copies[-1].start()
    for i in range(L_CHUNKS):
        at = pl.ds(i * rows_l, rows_l)
        l_copies.append(pltpu.make_async_copy(legendre_any.at[0, at], l_f32.at[at], l_sem.at[i]))

    barrier = pltpu.get_barrier_semaphore()
    for ids in peers:
        pl.semaphore_signal(barrier, inc=1, device_id=ids, device_id_type=MESH)

    for copy in w_copies[W_CHUNKS // 2 :]:
        copy.start()
    for copy in small:
        copy.wait()

    lane = iota((ORDERS, 128), 1)
    orders = jnp.zeros((ORDERS, 128), jnp.int32)
    for i in range(ORDERS):
        orders = jnp.where(iota((ORDERS, 128), 0) == i, window[i], orders)
    angle = ((orders * lane) & (NLON - 1)).astype(F32) * (2.0 * math.pi / NLON)
    table = jnp.concatenate([jnp.cos(angle), jnp.sin(angle)], axis=0)
    t_high, t_low = split(table)
    table_wide = jnp.concatenate([t_high, t_low, t_high], axis=1)
    turn = ((orders * col[...]) & 63).astype(F32) * (2.0 * math.pi / 64)
    turn_cos, turn_sin = jnp.cos(turn), jnp.sin(turn)

    owner = jnp.broadcast_to(dest[...], (TILES, TILES))
    earlier = (owner.T == owner) & (iota((TILES, TILES), 0) < iota((TILES, TILES), 1))
    slot = jnp.sum(jnp.where(earlier, 1.0, 0.0), axis=0, keepdims=True).astype(jnp.int32)
    place = slot * 16 + (dest[...] & 15)
    tile_band = dest[...] >> 4
    at_place = jnp.where(iota((256, TILES), 0) == tile_band * 32 + place, 1.0, 0.0).astype(BF16)
    code = jnp.broadcast_to((row[...] + 1).astype(F32), (ORDERS, TILES)).astype(BF16)
    own_lane = iota((GROUP, 128 * GROUP), 1) // 128 == iota((GROUP, 128 * GROUP), 0)

    def cells_of(i, _):
        tiles = pl.ds(pl.multiple_of(i * GROUP, 8), GROUP)
        values = thick[tiles]
        values = jnp.where(own_lane, jnp.concatenate([values] * GROUP, axis=1), 0.0)
        v_high, v_low = split(values)
        pieces = [split(w_f32[i * GROUP + t]) for t in range(GROUP)]
        right = jnp.concatenate([high for high, _ in pieces], axis=1)
        both = dot(jnp.concatenate([v_high, v_low], axis=0), right, NT)
        right = jnp.concatenate([low for _, low in pieces], axis=1)
        cells[tiles] = both[0:GROUP] + both[GROUP:] + dot(v_high, right, NT)
        return 0

    for i in range(W_CHUNKS):
        w_copies[i].wait()
        if i == W_CHUNKS // 2:
            for copy in l_copies:
                copy.start()
        n = rows_w // GROUP
        lax.fori_loop(i * n, (i + 1) * n, cells_of, 0, unroll=2)

    high, low = split(cells[...])
    raw = dot(table_wide, jnp.concatenate([high, high, low], axis=1), NT)
    scale = NLON ** (-0.5)
    part_cos = (raw[0:16] * turn_cos - raw[16:32] * turn_sin) * scale
    part_sin = (raw[16:32] * turn_cos + raw[0:16] * turn_sin) * scale

    high, low = split(jnp.concatenate([part_cos, part_sin], axis=0))
    packed = dot(jnp.concatenate([high, low, code], axis=0), at_place, NT)
    values = packed[0:32] + packed[32:64]
    codes = packed[64:80]
    zeros = jnp.zeros((ORDERS, 32), F32)
    for i in range(BANDS):
        cut = slice(32 * i, 32 * i + 32)
        send_a[ORDERS * i : ORDERS * (i + 1)] = jnp.concatenate(
            [values[0:16, cut], values[16:32, cut], codes[:, cut], zeros], axis=1
        )

    pl.semaphore_wait(barrier, DEVICES - 1)

    def to_all(source, target, send_sem, recv_sem):
        for peer_band, peer_order in peers:
            peer = peer_band * ORDERS + peer_order
            pltpu.make_async_remote_copy(
                src_ref=source.at[pl.ds(peer, 1)],
                dst_ref=target.at[pl.ds(me, 1)],
                send_sem=send_sem.at[0],
                recv_sem=recv_sem.at[0],
                device_id=(peer_band, peer_order),
                device_id_type=MESH,
            ).start()
        target[pl.ds(me, 1)] = source[pl.ds(me, 1)]

    def wait_all(ref, sem):
        others = ref.at[pl.ds(0, DEVICES - 1)]
        pltpu.make_async_copy(others, others, sem.at[0]).wait()

    to_all(send_a, recv_a, a_send, a_recv)

    group = iota((128, 1024), 1) // 32
    spread[...] = jnp.where(iota((128, 1024), 0) == 64 + group, 1.0, 0.0).astype(BF16)
    spot = iota((128, TILES), 0) & 63
    for i in range(BANDS):
        mine = tile_band == i
        for p in range(2):
            pick[128 * i : 128 * (i + 1), 128 * p : 128 * (p + 1)] = jnp.where(
                mine & (spot == p * 32 + place), 1.0, 0.0
            ).astype(BF16)
    factor = love[...].astype(F32) / 1000.0

    def split_rows(step, _):
        at = pl.ds(pl.multiple_of(step * 16, 16), 16)
        high, low = split(l_f32[at])
        l_hi[at] = high
        l_lo[at] = low
        return 0

    for i in range(L_CHUNKS):
        l_copies[i].wait()
        lax.fori_loop(i * rows_l // 16, (i + 1) * rows_l // 16, split_rows, 0, unroll=2)

    def split_turned(step, _):
        at = pl.ds(pl.multiple_of(step * 128, 128), 128)
        t_hi[at] = l_hi[:, at].T
        t_lo[at] = l_lo[:, at].T
        return 0

    lax.fori_loop(0, DEGREES // 256, split_turned, 0, unroll=2)

    wait_all(recv_a, a_recv)

    got = recv_a[...]
    code = dot(got.astype(BF16), spread[...], NN)
    wanted = ((iota((128, 1024), 1) & 31) + 1).astype(F32)
    chosen = jnp.where(code == wanted, 1.0, 0.0).astype(BF16)
    mask[...] = chosen
    high, low = split(got.T[0:64])
    sums = dot(jnp.concatenate([high, low], axis=0), chosen, NN)
    sums = sums[0:64] + sums[64:128]
    diagonal = iota((64, 1024), 0) & 31
    sums = jnp.where(diagonal == iota((64, 1024), 1) // 32, sums, 0.0)
    spectra = jnp.concatenate(
        [
            jnp.sum(sums[0:32], axis=0, keepdims=True),
            jnp.sum(sums[32:64], axis=0, keepdims=True),
        ],
        axis=0,
    )
    spectra = (spectra[:, 0:512] + spectra[:, 512:1024]) * quad[...]

    high, low = split(spectra)
    both = jnp.concatenate([high.astype(F32), low.astype(F32)], axis=0).astype(BF16)
    copies = []
    for k in range(X_CHUNKS):
        cut = pl.ds(k * X_COLS, X_COLS)
        share = dot(both, l_hi[:, cut], NN)
        share = share[0:2] + share[2:4] + dot(high, l_lo[:, cut], NN)
        shares[k, band] = share
        for dy, dc in BAND_OFFSETS:
            copy = pltpu.make_async_remote_copy(
                src_ref=shares.at[k, band],
                dst_ref=shares.at[k, band],
                send_sem=x_send.at[k],
                recv_sem=x_recv.at[k],
                device_id=(band_of[dy, dc], order),
                device_id_type=MESH,
            )
            copy.start()

    lax.fori_loop(DEGREES // 256, DEGREES // 128, split_turned, 0, unroll=2)

    fields = jnp.zeros((2, LAT_BAND), F32)
    for k in range(X_CHUNKS):
        cut = pl.ds(k * X_COLS, X_COLS)
        others = shares.at[k, pl.ds(0, BANDS - 1)]
        pltpu.make_async_copy(others, others, x_recv.at[k]).wait()
        total = shares[k, 0]
        for i in range(1, BANDS):
            total = total + shares[k, i]
        total = total * factor[:, k * X_COLS : (k + 1) * X_COLS]
        coef_ref[0, :, cut] = total
        high, low = split(total)
        both = jnp.concatenate([high.astype(F32), low.astype(F32)], axis=0).astype(BF16)
        term = dot(both, t_hi[cut], NN)
        fields = fields + (term[0:2] + term[2:4] + dot(high, t_lo[cut], NN))

    twice = jnp.concatenate([fields, fields], axis=1)
    twice = jnp.concatenate(
        [
            jnp.broadcast_to(twice[0:1], (32, 1024)),
            jnp.broadcast_to(twice[1:2], (32, 1024)),
        ],
        axis=0,
    )
    twice = jnp.where(diagonal == iota((64, 1024), 1) // 32, twice, 0.0)
    high, low = split(twice)
    send_b[...] = dot(mask[...], jnp.concatenate([high, low], axis=0), NT)
    to_all(send_b, recv_b, b_send, b_recv)

    def split_tiles(step, _):
        at = pl.ds(pl.multiple_of(step * 4, 4), 4)
        flat = pl.ds(pl.multiple_of(step * 512, 512), 512)
        high, low = split(w_f32[at].reshape(512, 128))
        w_hi[flat] = high
        w_lo[flat] = low
        return 0

    lax.fori_loop(0, TILES // 4, split_tiles, 0, unroll=2)

    for k in range(X_CHUNKS):
        others = shares.at[k, pl.ds(0, BANDS - 1)]
        pltpu.make_async_copy(others, others, x_send.at[k]).wait()
    wait_all(send_a, a_send)
    wait_all(recv_b, b_recv)

    back = recv_b[...].astype(BF16)
    back = jnp.concatenate([back[16 * i : 16 * (i + 1)] for i in range(BANDS)], axis=1)
    tile_fields = dot(back, pick[...], NN)
    f_cos, f_sin = tile_fields[:, 0:128], tile_fields[:, 128:256]
    scale = (2 * ORDERS) ** (-0.5)
    turned = jnp.concatenate(
        [
            (f_cos * turn_cos + f_sin * turn_sin) * scale,
            (f_sin * turn_cos - f_cos * turn_sin) * scale,
        ],
        axis=0,
    )
    high, low = split(turned.T)
    response = dot(
        jnp.concatenate([high, high, low], axis=1),
        jnp.concatenate([t_high, t_low, t_high], axis=0),
        NN,
    )
    own_lane = iota((8, 1024), 1) // 128 == iota((8, 1024), 0)
    for g in range(TILES // 8):
        values = response[8 * g : 8 * (g + 1)]
        values = jnp.where(own_lane, jnp.concatenate([values] * 8, axis=1), 0.0)
        v_high, v_low = split(values)
        flat = pl.ds(1024 * g, 1024)
        both = dot(jnp.concatenate([v_high, v_low], axis=0), w_hi[flat], NN)
        uplift_ref[8 * g : 8 * (g + 1)] = both[0:8] + both[8:16] + dot(v_high, w_lo[flat], NN)
    wait_all(send_b, b_send)


def hand_over(uplift_in, coef_in, uplift_out, coef_out):
    uplift_out[...] = uplift_in[...]
    coef_out[...] = coef_in[...]


def on_device(
    thickness,
    tile_weights,
    tile_dest,
    tile_row,
    tile_col,
    window,
    quad_weights,
    legendre,
    love_code,
):
    hbm = pl.BlockSpec(memory_space=pltpu.HBM)
    vmem = pl.BlockSpec(memory_space=pltpu.VMEM)
    uplift, coefficients = pl.pallas_call(
        body,
        out_shape=(
            jax.ShapeDtypeStruct((TILES, 128), F32),
            jax.ShapeDtypeStruct((1, 2, DEGREES), F32),
        ),
        in_specs=[hbm] * 9,
        out_specs=(vmem, vmem),
        scratch_shapes=[
            pltpu.VMEM((TILES, 128), F32),
            pltpu.VMEM((1, TILES), jnp.int32),
            pltpu.VMEM((1, TILES), jnp.int32),
            pltpu.VMEM((1, TILES), jnp.int32),
            pltpu.SMEM((ORDERS,), jnp.int32),
            pltpu.VMEM((1, LAT_BAND), F32),
            pltpu.VMEM((1, DEGREES), jnp.int32),
            pltpu.VMEM((TILES, 128, 128), F32),
            pltpu.VMEM((TILES * 128, 128), BF16),
            pltpu.VMEM((TILES * 128, 128), BF16),
            pltpu.VMEM((LAT_BAND, DEGREES), F32),
            pltpu.VMEM((LAT_BAND, DEGREES), BF16),
            pltpu.VMEM((LAT_BAND, DEGREES), BF16),
            pltpu.VMEM((DEGREES, LAT_BAND), BF16),
            pltpu.VMEM((DEGREES, LAT_BAND), BF16),
            pltpu.VMEM((TILES, 128), F32),
            pltpu.VMEM((DEVICES, 128), F32),
            pltpu.VMEM((DEVICES, 128), F32),
            pltpu.VMEM((X_CHUNKS, BANDS, 2, X_COLS), F32),
            pltpu.VMEM((DEVICES, 128), F32),
            pltpu.VMEM((DEVICES, 128), F32),
            pltpu.VMEM((128, 1024), BF16),
            pltpu.VMEM((128, 1024), BF16),
            pltpu.VMEM((1024, 256), BF16),
            pltpu.SemaphoreType.DMA((7,)),
            pltpu.SemaphoreType.DMA((W_CHUNKS,)),
            pltpu.SemaphoreType.DMA((L_CHUNKS,)),
            pltpu.SemaphoreType.DMA((1,)),
            pltpu.SemaphoreType.DMA((1,)),
            pltpu.SemaphoreType.DMA((X_CHUNKS,)),
            pltpu.SemaphoreType.DMA((X_CHUNKS,)),
            pltpu.SemaphoreType.DMA((1,)),
            pltpu.SemaphoreType.DMA((1,)),
        ],
        compiler_params=pltpu.CompilerParams(
            collective_id=0, has_side_effects=True, vmem_limit_bytes=62 * 1024 * 1024
        ),
    )(
        thickness.reshape(TILES, 128),
        tile_weights,
        tile_dest.reshape(1, TILES),
        tile_row.reshape(1, TILES),
        tile_col.reshape(1, TILES),
        window,
        quad_weights.reshape(1, LAT_BAND),
        legendre,
        love_code.reshape(1, DEGREES),
    )
    uplift, coefficients = pl.pallas_call(
        hand_over,
        out_shape=(
            jax.ShapeDtypeStruct((TILES, 128), F32),
            jax.ShapeDtypeStruct((1, 2, DEGREES), F32),
        ),
        in_specs=[vmem, vmem],
        out_specs=(vmem, vmem),
        compiler_params=pltpu.CompilerParams(vmem_limit_bytes=62 * 1024 * 1024),
    )(uplift, coefficients)
    return uplift.reshape(TILES * 128), coefficients


def solution(mesh):
    return jax.shard_map(
        on_device,
        mesh=mesh,
        in_specs=(
            P(("band", "order")),
            P(("band", "order"), None, None),
            P(("band", "order"), None),
            P(("band", "order")),
            P(("band", "order")),
            P(),
            P("band"),
            P("order", "band", None),
            P(),
        ),
        out_specs=(P(("band", "order")), P("order", None, None)),
        check_vma=False,
    )
```

```python
import math

import jax
import jax.numpy as jnp
from jax import lax
from jax.experimental import pallas as pl
from jax.experimental.pallas import tpu as pltpu
from jax.sharding import PartitionSpec as P

NLON = 8192
F32 = jnp.float32
BF16 = jnp.bfloat16
MESH = pl.DeviceIdType.MESH
NN = (((1,), (0,)), ((), ()))
NT = (((1,), (1,)), ((), ()))

BANDS = 8
ORDERS = 16
DEVICES = BANDS * ORDERS
TILES = 128
DEGREES = 4096
LAT_BAND = 512
LAT_DEV = 32
W_CHUNKS = 4
GROUP = 16
L_CHUNKS = 4
X_CHUNKS = 4
X_COLS = DEGREES // X_CHUNKS


def ring(k):
    return min(k, 4 - k)


OFFSETS = sorted(
    [
        (dy, dc, dz, dx)
        for dy in range(4)
        for dc in range(2)
        for dz in range(4)
        for dx in range(4)
        if (dy, dc, dz, dx) != (0, 0, 0, 0)
    ],
    key=lambda o: -(ring(o[0]) + ring(o[2]) + ring(o[3]) + 0.3 * o[1]),
)
BAND_OFFSETS = sorted(
    [(dy, dc) for dy in range(4) for dc in range(2) if (dy, dc) != (0, 0)],
    key=lambda o: -(ring(o[0]) + 0.3 * o[1]),
)


def dot(a, b, dims):
    return lax.dot_general(a, b, dims, preferred_element_type=F32)


def split(x):
    high = x.astype(BF16)
    low = (x - high.astype(F32)).astype(BF16)
    return high, low


def cosine(phase):
    away = jnp.minimum(phase, NLON - phase)
    near = jnp.minimum(away, NLON // 2 - away)
    x = near.astype(F32) * (2.0 * math.pi / NLON)
    square = x * x
    value = jnp.full(phase.shape, -1.0 / math.factorial(14), F32)
    for n in (12, 10, 8, 6, 4, 2, 0):
        value = value * square + (-1.0) ** (n // 2) / math.factorial(n)
    return jnp.where(away > NLON // 4, -value, value)


def iota(shape, dim):
    return lax.broadcasted_iota(jnp.int32, shape, dim)


def body(
    thick_any,
    weights_any,
    dest_any,
    row_any,
    col_any,
    window_any,
    quad_any,
    legendre_any,
    love_any,
    uplift_ref,
    coef_ref,
    thick,
    dest,
    row,
    col,
    window,
    quad,
    love,
    w_f32,
    w_hi,
    w_lo,
    l_f32,
    l_hi,
    l_lo,
    t_hi,
    t_lo,
    cells,
    send_a,
    recv_a,
    shares,
    send_b,
    recv_b,
    spread,
    mask,
    pick,
    small_sem,
    w_sem,
    l_sem,
    a_send,
    a_recv,
    x_send,
    x_recv,
    b_send,
    b_recv,
):
    band = lax.axis_index("band")
    order = lax.axis_index("order")
    me = band * ORDERS + order
    y, core, z, x = band // 2, band % 2, order // 4, order % 4
    band_of = {(i, j): ((y + i) % 4) * 2 + (core + j) % 2 for i in range(4) for j in range(2)}
    order_of = {(i, j): ((z + i) % 4) * 4 + (x + j) % 4 for i in range(4) for j in range(4)}
    peers = [(band_of[dy, dc], order_of[dz, dx]) for dy, dc, dz, dx in OFFSETS]

    rows_w = TILES // W_CHUNKS
    rows_l = LAT_BAND // L_CHUNKS
    small = []
    for i, (source, target) in enumerate(
        (
            (thick_any, thick),
            (dest_any, dest),
            (row_any, row),
            (col_any, col),
            (window_any, window),
            (quad_any, quad),
            (love_any, love),
        )
    ):
        small.append(pltpu.make_async_copy(source, target, small_sem.at[i]))
        small[-1].start()
    w_copies, l_copies = [], []
    for i in range(W_CHUNKS):
        at = pl.ds(i * rows_w, rows_w)
        w_copies.append(pltpu.make_async_copy(weights_any.at[at], w_f32.at[at], w_sem.at[i]))
        if i < W_CHUNKS // 2:
            w_copies[-1].start()
    for i in range(L_CHUNKS):
        at = pl.ds(i * rows_l, rows_l)
        l_copies.append(pltpu.make_async_copy(legendre_any.at[0, at], l_f32.at[at], l_sem.at[i]))

    barrier = pltpu.get_barrier_semaphore()
    for ids in peers:
        pl.semaphore_signal(barrier, inc=1, device_id=ids, device_id_type=MESH)

    w_copies[2].start()
    for copy in small:
        copy.wait()

    lane = iota((ORDERS, 128), 1)
    orders = jnp.zeros((ORDERS, 128), jnp.int32)
    for i in range(ORDERS):
        orders = jnp.where(iota((ORDERS, 128), 0) == i, window[i], orders)
    turn = ((orders * col[...]) & 63) * (NLON // 64)
    phase = jnp.concatenate([(orders * lane) & (NLON - 1), turn], axis=0)
    phase = jnp.concatenate([phase, (phase + 3 * NLON // 4) & (NLON - 1)], axis=0)
    waves = cosine(phase)
    table = jnp.concatenate([waves[0:16], waves[32:48]], axis=0)
    turn_cos, turn_sin = waves[16:32], waves[48:64]
    t_high, t_low = split(table)
    table_wide = jnp.concatenate([t_high, t_low, t_high], axis=1)

    owner = jnp.broadcast_to(dest[...], (TILES, TILES))
    earlier = (owner.T == owner) & (iota((TILES, TILES), 0) < iota((TILES, TILES), 1))
    slot = jnp.sum(jnp.where(earlier, 1.0, 0.0), axis=0, keepdims=True).astype(jnp.int32)
    place = slot * 16 + (dest[...] & 15)
    tile_band = dest[...] >> 4
    at_place = jnp.where(iota((256, TILES), 0) == tile_band * 32 + place, 1.0, 0.0).astype(BF16)
    code = jnp.broadcast_to((row[...] + 1).astype(F32), (ORDERS, TILES)).astype(BF16)
    w_copies[3].start()

    own_lane = iota((GROUP, 128 * GROUP), 1) // 128 == iota((GROUP, 128 * GROUP), 0)

    def cells_of(i, _):
        tiles = pl.ds(pl.multiple_of(i * GROUP, 8), GROUP)
        values = thick[tiles]
        values = jnp.where(own_lane, jnp.concatenate([values] * GROUP, axis=1), 0.0)
        v_high, v_low = split(values)
        pieces = [split(w_f32[i * GROUP + t]) for t in range(GROUP)]
        right = jnp.concatenate([high for high, _ in pieces], axis=1)
        both = dot(jnp.concatenate([v_high, v_low], axis=0), right, NT)
        right = jnp.concatenate([low for _, low in pieces], axis=1)
        cells[tiles] = both[0:GROUP] + both[GROUP:] + dot(v_high, right, NT)
        return 0

    for i in range(W_CHUNKS):
        w_copies[i].wait()
        if i == W_CHUNKS - 1:
            for copy in l_copies:
                copy.start()
        n = rows_w // GROUP
        lax.fori_loop(i * n, (i + 1) * n, cells_of, 0, unroll=2)

    high, low = split(cells[...])
    raw = dot(table_wide, jnp.concatenate([high, high, low], axis=1), NT)
    scale = NLON ** (-0.5)
    part_cos = (raw[0:16] * turn_cos - raw[16:32] * turn_sin) * scale
    part_sin = (raw[16:32] * turn_cos + raw[0:16] * turn_sin) * scale

    high, low = split(jnp.concatenate([part_cos, part_sin], axis=0))
    packed = dot(jnp.concatenate([high, low, code], axis=0), at_place, NT)
    values = packed[0:32] + packed[32:64]
    codes = packed[64:80]
    zeros = jnp.zeros((ORDERS, 32), F32)
    for i in range(BANDS):
        cut = slice(32 * i, 32 * i + 32)
        send_a[ORDERS * i : ORDERS * (i + 1)] = jnp.concatenate(
            [values[0:16, cut], values[16:32, cut], codes[:, cut], zeros], axis=1
        )

    pl.semaphore_wait(barrier, DEVICES - 1)

    def to_all(source, target, send_sem, recv_sem):
        for peer_band, peer_order in peers:
            peer = peer_band * ORDERS + peer_order
            pltpu.make_async_remote_copy(
                src_ref=source.at[pl.ds(peer, 1)],
                dst_ref=target.at[pl.ds(me, 1)],
                send_sem=send_sem.at[0],
                recv_sem=recv_sem.at[0],
                device_id=(peer_band, peer_order),
                device_id_type=MESH,
            ).start()
        target[pl.ds(me, 1)] = source[pl.ds(me, 1)]

    def wait_all(ref, sem):
        others = ref.at[pl.ds(0, DEVICES - 1)]
        pltpu.make_async_copy(others, others, sem.at[0]).wait()

    to_all(send_a, recv_a, a_send, a_recv)

    group = iota((128, 1024), 1) // 32
    spread[...] = jnp.where(iota((128, 1024), 0) == 64 + group, 1.0, 0.0).astype(BF16)
    spot = iota((128, TILES), 0) & 63
    for i in range(BANDS):
        mine = tile_band == i
        for p in range(2):
            pick[128 * i : 128 * (i + 1), 128 * p : 128 * (p + 1)] = jnp.where(
                mine & (spot == p * 32 + place), 1.0, 0.0
            ).astype(BF16)
    factor = love[...].astype(F32) / 1000.0

    def split_rows(step, _):
        at = pl.ds(pl.multiple_of(step * 16, 16), 16)
        high, low = split(l_f32[at])
        l_hi[at] = high
        l_lo[at] = low
        return 0

    for i in range(L_CHUNKS):
        l_copies[i].wait()
        lax.fori_loop(i * rows_l // 16, (i + 1) * rows_l // 16, split_rows, 0, unroll=2)

    def split_turned(step, _):
        at = pl.ds(pl.multiple_of(step * 128, 128), 128)
        t_hi[at] = l_hi[:, at].T
        t_lo[at] = l_lo[:, at].T
        return 0

    lax.fori_loop(0, DEGREES // 256, split_turned, 0, unroll=2)

    wait_all(recv_a, a_recv)

    got = recv_a[...]
    code = dot(got.astype(BF16), spread[...], NN)
    wanted = ((iota((128, 1024), 1) & 31) + 1).astype(F32)
    chosen = jnp.where(code == wanted, 1.0, 0.0).astype(BF16)
    mask[...] = chosen
    high, low = split(got.T[0:64])
    sums = dot(jnp.concatenate([high, low], axis=0), chosen, NN)
    sums = sums[0:64] + sums[64:128]
    diagonal = iota((64, 1024), 0) & 31
    sums = jnp.where(diagonal == iota((64, 1024), 1) // 32, sums, 0.0)
    spectra = jnp.concatenate(
        [
            jnp.sum(sums[0:32], axis=0, keepdims=True),
            jnp.sum(sums[32:64], axis=0, keepdims=True),
        ],
        axis=0,
    )
    spectra = (spectra[:, 0:512] + spectra[:, 512:1024]) * quad[...]

    high, low = split(spectra)
    both = jnp.concatenate([high.astype(F32), low.astype(F32)], axis=0).astype(BF16)
    copies = []
    for k in range(X_CHUNKS):
        cut = pl.ds(k * X_COLS, X_COLS)
        share = dot(both, l_hi[:, cut], NN)
        share = share[0:2] + share[2:4] + dot(high, l_lo[:, cut], NN)
        shares[k, band] = share
        for dy, dc in BAND_OFFSETS:
            copy = pltpu.make_async_remote_copy(
                src_ref=shares.at[k, band],
                dst_ref=shares.at[k, band],
                send_sem=x_send.at[k],
                recv_sem=x_recv.at[k],
                device_id=(band_of[dy, dc], order),
                device_id_type=MESH,
            )
            copy.start()

    lax.fori_loop(DEGREES // 256, DEGREES // 128, split_turned, 0, unroll=2)

    fields = jnp.zeros((2, LAT_BAND), F32)
    for k in range(X_CHUNKS):
        cut = pl.ds(k * X_COLS, X_COLS)
        others = shares.at[k, pl.ds(0, BANDS - 1)]
        pltpu.make_async_copy(others, others, x_recv.at[k]).wait()
        total = shares[k, 0]
        for i in range(1, BANDS):
            total = total + shares[k, i]
        total = total * factor[:, k * X_COLS : (k + 1) * X_COLS]
        coef_ref[0, :, cut] = total
        high, low = split(total)
        both = jnp.concatenate([high.astype(F32), low.astype(F32)], axis=0).astype(BF16)
        term = dot(both, t_hi[cut], NN)
        fields = fields + (term[0:2] + term[2:4] + dot(high, t_lo[cut], NN))

    twice = jnp.concatenate([fields, fields], axis=1)
    twice = jnp.concatenate(
        [
            jnp.broadcast_to(twice[0:1], (32, 1024)),
            jnp.broadcast_to(twice[1:2], (32, 1024)),
        ],
        axis=0,
    )
    twice = jnp.where(diagonal == iota((64, 1024), 1) // 32, twice, 0.0)
    high, low = split(twice)
    send_b[...] = dot(mask[...], jnp.concatenate([high, low], axis=0), NT)
    to_all(send_b, recv_b, b_send, b_recv)

    def split_tiles(step, _):
        at = pl.ds(pl.multiple_of(step * 4, 4), 4)
        flat = pl.ds(pl.multiple_of(step * 512, 512), 512)
        high, low = split(w_f32[at].reshape(512, 128))
        w_hi[flat] = high
        w_lo[flat] = low
        return 0

    lax.fori_loop(0, TILES // 4, split_tiles, 0, unroll=2)

    for k in range(X_CHUNKS):
        others = shares.at[k, pl.ds(0, BANDS - 1)]
        pltpu.make_async_copy(others, others, x_send.at[k]).wait()
    wait_all(send_a, a_send)
    wait_all(recv_b, b_recv)

    back = recv_b[...].astype(BF16)
    back = jnp.concatenate([back[16 * i : 16 * (i + 1)] for i in range(BANDS)], axis=1)
    tile_fields = dot(back, pick[...], NN)
    f_cos, f_sin = tile_fields[:, 0:128], tile_fields[:, 128:256]
    scale = (2 * ORDERS) ** (-0.5)
    turned = jnp.concatenate(
        [
            (f_cos * turn_cos + f_sin * turn_sin) * scale,
            (f_sin * turn_cos - f_cos * turn_sin) * scale,
        ],
        axis=0,
    )
    high, low = split(turned.T)
    response = dot(
        jnp.concatenate([high, high, low], axis=1),
        jnp.concatenate([t_high, t_low, t_high], axis=0),
        NN,
    )
    own_lane = iota((8, 1024), 1) // 128 == iota((8, 1024), 0)
    for g in range(TILES // 8):
        values = response[8 * g : 8 * (g + 1)]
        values = jnp.where(own_lane, jnp.concatenate([values] * 8, axis=1), 0.0)
        v_high, v_low = split(values)
        flat = pl.ds(1024 * g, 1024)
        both = dot(jnp.concatenate([v_high, v_low], axis=0), w_hi[flat], NN)
        uplift_ref[8 * g : 8 * (g + 1)] = both[0:8] + both[8:16] + dot(v_high, w_lo[flat], NN)
    wait_all(send_b, b_send)


def hand_over(uplift_in, coef_in, uplift_out, coef_out):
    uplift_out[...] = uplift_in[...]
    coef_out[...] = coef_in[...]


def on_device(
    thickness,
    tile_weights,
    tile_dest,
    tile_row,
    tile_col,
    window,
    quad_weights,
    legendre,
    love_code,
):
    hbm = pl.BlockSpec(memory_space=pltpu.HBM)
    vmem = pl.BlockSpec(memory_space=pltpu.VMEM)
    uplift, coefficients = pl.pallas_call(
        body,
        out_shape=(
            jax.ShapeDtypeStruct((TILES, 128), F32),
            jax.ShapeDtypeStruct((1, 2, DEGREES), F32),
        ),
        in_specs=[hbm] * 9,
        out_specs=(vmem, vmem),
        scratch_shapes=[
            pltpu.VMEM((TILES, 128), F32),
            pltpu.VMEM((1, TILES), jnp.int32),
            pltpu.VMEM((1, TILES), jnp.int32),
            pltpu.VMEM((1, TILES), jnp.int32),
            pltpu.SMEM((ORDERS,), jnp.int32),
            pltpu.VMEM((1, LAT_BAND), F32),
            pltpu.VMEM((1, DEGREES), jnp.int32),
            pltpu.VMEM((TILES, 128, 128), F32),
            pltpu.VMEM((TILES * 128, 128), BF16),
            pltpu.VMEM((TILES * 128, 128), BF16),
            pltpu.VMEM((LAT_BAND, DEGREES), F32),
            pltpu.VMEM((LAT_BAND, DEGREES), BF16),
            pltpu.VMEM((LAT_BAND, DEGREES), BF16),
            pltpu.VMEM((DEGREES, LAT_BAND), BF16),
            pltpu.VMEM((DEGREES, LAT_BAND), BF16),
            pltpu.VMEM((TILES, 128), F32),
            pltpu.VMEM((DEVICES, 128), F32),
            pltpu.VMEM((DEVICES, 128), F32),
            pltpu.VMEM((X_CHUNKS, BANDS, 2, X_COLS), F32),
            pltpu.VMEM((DEVICES, 128), F32),
            pltpu.VMEM((DEVICES, 128), F32),
            pltpu.VMEM((128, 1024), BF16),
            pltpu.VMEM((128, 1024), BF16),
            pltpu.VMEM((1024, 256), BF16),
            pltpu.SemaphoreType.DMA((7,)),
            pltpu.SemaphoreType.DMA((W_CHUNKS,)),
            pltpu.SemaphoreType.DMA((L_CHUNKS,)),
            pltpu.SemaphoreType.DMA((1,)),
            pltpu.SemaphoreType.DMA((1,)),
            pltpu.SemaphoreType.DMA((X_CHUNKS,)),
            pltpu.SemaphoreType.DMA((X_CHUNKS,)),
            pltpu.SemaphoreType.DMA((1,)),
            pltpu.SemaphoreType.DMA((1,)),
        ],
        compiler_params=pltpu.CompilerParams(
            collective_id=0, has_side_effects=True, vmem_limit_bytes=62 * 1024 * 1024
        ),
    )(
        thickness.reshape(TILES, 128),
        tile_weights,
        tile_dest.reshape(1, TILES),
        tile_row.reshape(1, TILES),
        tile_col.reshape(1, TILES),
        window,
        quad_weights.reshape(1, LAT_BAND),
        legendre,
        love_code.reshape(1, DEGREES),
    )
    uplift, coefficients = pl.pallas_call(
        hand_over,
        out_shape=(
            jax.ShapeDtypeStruct((TILES, 128), F32),
            jax.ShapeDtypeStruct((1, 2, DEGREES), F32),
        ),
        in_specs=[vmem, vmem],
        out_specs=(vmem, vmem),
        compiler_params=pltpu.CompilerParams(vmem_limit_bytes=62 * 1024 * 1024),
    )(uplift, coefficients)
    return uplift.reshape(TILES * 128), coefficients


def solution(mesh):
    return jax.shard_map(
        on_device,
        mesh=mesh,
        in_specs=(
            P(("band", "order")),
            P(("band", "order"), None, None),
            P(("band", "order"), None),
            P(("band", "order")),
            P(("band", "order")),
            P(),
            P("band"),
            P("order", "band", None),
            P(),
        ),
        out_specs=(P(("band", "order")), P("order", None, None)),
        check_vma=False,
    )
```
